32 devices in a mesh: section: 2 (over x), dp: 8 (over z, y), tensor: 2 (over core).
Axes of the slice: x: 2, y: 2, z: 4, core: 2. Of those that a mesh axis runs over, the one named last changes fastest.
Arguments:
- hidden: bfloat16 [2, 128, 7168], P('section', ('dp', 'tensor')), may hold values from -90 to 90
- gain: float32 [7168], replicated, may hold values from 0.5 to 1.5
- table: bfloat16 [65536, 7168], P(('dp', 'tensor')), may hold values from -4 to 4
- labels: int32 [2, 128], P('section'), may hold values from 0 to 65535
- token_weight: float32 [2, 128], P('section'), may hold values from 4 to 32
Outputs:
- grad_input: bfloat16 [2, 128, 7168], P('section', ('dp', 'tensor'))
- table_grad: bfloat16 [65536, 7168], P(('dp', 'tensor'), 'section')
The draws below stay inside these ranges and needn't reach their ends.
All inputs are finite; a program needn't handle non-finite values.
Results may differ from the reference program's by a relative error of at most 0.0058.
Values may be sent and summed in bfloat16 or wider, within the bound.
A program may use at most 512 MiB of HBM per device.

```python
import math
import jax
import jax.numpy as jnp
from jax import lax

D = 7168
VOCAB = 65536
TOKENS = 128


common_weight = 1.5


def hidden_base(key):
    first_key, second_key, third_key, fourth_key = jax.random.split(key, 4)
    normal_part = jax.random.truncated_normal(first_key, -5.0, 5.0, (2, TOKENS, D), jnp.float32)
    common_part = jax.random.truncated_normal(fourth_key, -3.0, 3.0, (D,), jnp.float32)
    columns = jnp.exp(jax.random.uniform(second_key, (D,), jnp.float32, math.log(0.3), math.log(3.0)))
    row_scale = jnp.exp(jax.random.uniform(third_key, (2, TOKENS, 1), jnp.float32, math.log(0.3), math.log(3.0)))
    rows = (normal_part + common_weight * common_part) * columns * row_scale
    return rows


def draw_hidden(key, part):
    shared_rows = hidden_base(key)
    return shared_rows.astype(jnp.bfloat16)


def draw_table(key, part):
    key = jax.random.fold_in(key, 7)
    keys = jax.random.split(key, 2)
    ramp = jnp.arange(VOCAB, dtype=jnp.float32) / VOCAB
    roughness = jnp.exp(jax.random.uniform(keys[0], (VOCAB,), jnp.float32, math.log(0.8), math.log(1.25)))
    row_size = (2.5 + ramp) * roughness / math.sqrt(D)
    entries = jax.random.truncated_normal(keys[1], -6.0, 6.0, (VOCAB, D), jnp.float32) * row_size[:, None]
    return entries.astype(jnp.bfloat16)


def set_ends(drawn, key, smallest, largest):
    longest = drawn.shape.index(max(drawn.shape))
    spots = []
    for shift in (0, 1):
        where = [jax.random.randint(jax.random.fold_in(key, axis), (), 0, length) for axis, length in enumerate(drawn.shape)]
        where[longest] = (where[longest] + shift) % drawn.shape[longest]
        spots.append(tuple(where))
    return drawn.at[spots[0]].set(smallest).at[spots[1]].set(largest)


def steps_of(rng, extent, pieces, smallest, largest):
    loudness, own = 1.0, jax.random.fold_in(rng, 6)
    for position, shards_of in pieces:
        heights = jnp.exp(jax.random.uniform(jax.random.fold_in(own, position), (shards_of,), jnp.float32, smallest / len(pieces), largest / len(pieces)))
        loudness = loudness * jnp.repeat(heights, extent[position] // shards_of).reshape([-1 if axis == position else 1 for axis in range(len(extent))])
    return loudness


def setup_inputs(seed: int = 0) -> dict:
    splits = jax.random.split(jax.random.key(seed), 6)
    hidden = draw_hidden(jax.random.fold_in(splits[5], 71), 0)
    gain = jnp.clip(1.0 + 0.1 * jax.random.normal(splits[1], (D,), jnp.float32), 0.5, 1.5)
    table = draw_table(jax.random.fold_in(splits[5], 71), 0)
    labels = set_ends(jax.random.randint(splits[3], (2, TOKENS), 0, VOCAB), jax.random.fold_in(splits[3], 1), 0, VOCAB - 1).astype(jnp.int32)
    token_weight = jnp.clip(jnp.exp(math.log(32.0) - 2.0794415 * jax.random.uniform(splits[4], (2, TOKENS), jnp.float32) ** steps_of(splits[4], (2, TOKENS), ((0, 2),), -0.2, 0.2)), 4.0, 32.0)
    return {"hidden": hidden, "gain": gain, "table": table, "labels": labels, "token_weight": token_weight}


def reference(hidden, gain, table, labels, token_weight):
    rows = hidden.reshape(2 * TOKENS, D).astype(jnp.float32)
    inverse_rms = lax.rsqrt(lax.optimization_barrier(jnp.mean(rows * rows, axis=1, keepdims=True)) + 1e-06)
    unit_rows = rows * inverse_rms
    normed = (unit_rows * gain).astype(jnp.bfloat16)
    normed_wide = normed.astype(jnp.float32)
    block_rows = min(VOCAB, 4096)
    block_count = VOCAB // block_rows
    table_blocks = table.reshape(block_count, block_rows, D)

    def logit_block(block):
        return jnp.dot(normed_wide, block.astype(jnp.float32).T, preferred_element_type=jnp.float32)
    logit_parts = lax.map(logit_block, table_blocks)
    logits = jnp.transpose(logit_parts, (1, 0, 2)).reshape(2 * TOKENS, VOCAB)
    row_peak = lax.optimization_barrier(jnp.max(logits, axis=1, keepdims=True))
    log_total = row_peak + jnp.log(lax.optimization_barrier(jnp.sum(jnp.exp(logits - row_peak), axis=1, keepdims=True)))
    entries = jnp.arange(VOCAB, dtype=jnp.int32)
    is_label = (entries[None, :] == labels.reshape(-1).astype(jnp.int32)[:, None]).astype(jnp.float32)
    weights = token_weight.reshape(-1, 1)
    logit_grad = (weights * (jnp.exp(logits - log_total) - is_label)).astype(jnp.bfloat16)
    grad_blocks = logit_grad.T.reshape(block_count, block_rows, 2 * TOKENS)

    def accumulate(total, pair):
        grad_block, table_block = pair
        term = jnp.dot(grad_block.astype(jnp.float32).T, table_block.astype(jnp.float32), preferred_element_type=jnp.float32)
        return (total + term, None)
    normed_grad, unused = lax.scan(accumulate, jnp.zeros((2 * TOKENS, D), jnp.float32), (grad_blocks, table_blocks))
    scaled = normed_grad * gain
    section_grad = (inverse_rms * (scaled - unit_rows * lax.optimization_barrier(jnp.mean(scaled * unit_rows, axis=1, keepdims=True)))).astype(jnp.bfloat16)
    grad_input = section_grad.reshape(2, TOKENS, D)[::-1]

    def table_block(block):
        return jnp.dot(block.astype(jnp.float32), normed_wide, preferred_element_type=jnp.float32).astype(jnp.bfloat16)
    table_grad = lax.map(table_block, grad_blocks).reshape(VOCAB, D)
    return (grad_input, table_grad)
```

```python
import jax
import jax.numpy as jnp
from jax import lax
from jax.sharding import PartitionSpec as P


def normalize(source_rows, gain):
    values = source_rows.astype(jnp.float32)
    inverse = lax.rsqrt(jnp.mean(values * values, axis=1, keepdims=True) + 1e-06)
    unit = values * inverse
    return (inverse, unit, (unit * gain).astype(jnp.bfloat16))


def on_device(hidden, gain, table, labels, token_weight):
    section = lax.axis_index("section")
    tokens = labels.shape[1]
    vocab_rows, width = table.shape
    half = width // 2
    normed_own = normalize(hidden[0], gain)[2]
    normed = lax.all_gather(normed_own, ("section", "dp", "tensor"), axis=0, tiled=True)
    other_rows = lax.ppermute(hidden[0], "section", [(0, 1), (1, 0)])
    labels_all = lax.all_gather(labels[0], "section", axis=0, tiled=True)
    weight_all = lax.all_gather(token_weight[0], "section", axis=0, tiled=True)
    logits = jnp.einsum("td,vd->tv", normed, table, preferred_element_type=jnp.float32)
    peak = jnp.max(logits, axis=1)
    part = jnp.sum(jnp.exp(logits - peak[:, None]), axis=1)
    stats = lax.all_gather(jnp.stack([peak, part]), ("dp", "tensor"), axis=0)
    row_peak = jnp.max(stats[:, 0], axis=0)
    row_sum = jnp.sum(stats[:, 1] * jnp.exp(stats[:, 0] - row_peak[None]), axis=0)
    log_total = row_peak + jnp.log(row_sum)
    first_entry = lax.axis_index(("dp", "tensor")) * vocab_rows
    entries = first_entry + jnp.arange(vocab_rows, dtype=jnp.int32)
    is_label = (entries[None, :] == labels_all[:, None]).astype(jnp.float32)
    logit_grad = (
        weight_all[:, None] * (jnp.exp(logits - log_total[:, None]) - is_label)
    ).astype(jnp.bfloat16)
    other_grad = lax.dynamic_slice_in_dim(logit_grad, (1 - section) * tokens, tokens, axis=0)
    normed_grad = lax.psum_scatter(
        jnp.dot(other_grad, table, preferred_element_type=jnp.float32),
        ("dp", "tensor"),
        scatter_dimension=0,
        tiled=True,
    )
    own_columns = lax.dynamic_slice_in_dim(normed, section * half, half, axis=1)
    table_grad = jnp.einsum(
        "tv,td->vd", logit_grad, own_columns, preferred_element_type=jnp.float32
    ).astype(jnp.bfloat16)
    inverse, unit, _ = normalize(other_rows, gain)
    scaled = normed_grad * gain
    section_grad = (
        inverse * (scaled - unit * jnp.mean(scaled * unit, axis=1, keepdims=True))
    ).astype(jnp.bfloat16)
    return (section_grad[None], table_grad)


def solution(mesh):
    in_specs = (
        P("section", ("dp", "tensor"), None),
        P(),
        P(("dp", "tensor"), None),
        P("section", None),
        P("section", None),
    )
    out_specs = (P("section", ("dp", "tensor"), None), P(("dp", "tensor"), "section"))
    return jax.shard_map(
        on_device, mesh=mesh, in_specs=in_specs, out_specs=out_specs, check_vma=False
    )
```

```python
import jax
import jax.numpy as jnp
from jax import lax
from jax.experimental import pallas as pl
from jax.experimental.pallas import tpu as pltpu
from jax.sharding import PartitionSpec as P


def normalize(source_rows, gain):
    values = source_rows.astype(jnp.float32)
    inverse = lax.rsqrt(jnp.mean(values * values, axis=1, keepdims=True) + 1e-06)
    unit = values * inverse
    return (inverse, unit, (unit * gain).astype(jnp.bfloat16))


MESH = pl.DeviceIdType.MESH
PAIR = 1024
SLAB = 512
SLOTS = 4
TILE = 512


def fused_kernel(
    hidden_ref, gain_ref, table_ref, marks_ref,
    grad_out, rows_out, sum_out,
    rows, both, other_marks, ring, logits, grad_t, grad_o, stat_out, stat_in,
    mine, sent, got, y_part, y_sent, y_got, z_sent, z_got, final, cross,
    ring_sem, out_sem, pair_sem, mark_sem, z_sem, near_sem, sib_sem, stat_sem,
    back_sem, last_sem,
):
    x = lax.axis_index("section")
    dp = lax.axis_index("dp")
    core = lax.axis_index("tensor")
    z, y = dp // 2, dp % 2
    pairs = table_ref.shape[1] // PAIR
    vocab = table_ref.shape[0]
    half = rows_out.shape[4]
    tiles = vocab // TILE

    sibling = {"tensor": 1 - core}
    across = {"section": 1 - x}
    beside = {"dp": z * 2 + (1 - y)}

    def along(step):
        return {"dp": ((z + step) % 4) * 2 + y}

    def load(pair):
        return pltpu.make_async_copy(
            table_ref.at[:, pl.ds(pl.multiple_of(pair * PAIR, PAIR), PAIR)],
            ring.at[pair % SLOTS],
            ring_sem.at[pair % SLOTS],
        )

    for pair in range(SLOTS):
        load(pair).start()

    def remote(src, dst, send, recv, device):
        return pltpu.make_async_remote_copy(
            src_ref=src, dst_ref=dst, send_sem=send, recv_sem=recv,
            device_id=device, device_id_type=MESH,
        )

    barrier = pltpu.get_barrier_semaphore()
    peers = [sibling, across, beside, along(1), along(2), along(3)]
    for peer in peers:
        pl.semaphore_signal(barrier, inc=1, device_id=peer, device_id_type=MESH)

    values = hidden_ref[...].astype(jnp.float32)
    inverse = lax.rsqrt(jnp.mean(values * values, axis=1, keepdims=True) + 1e-06)
    normed = (values * inverse * gain_ref[...]).astype(jnp.bfloat16)
    both[core] = normed.astype(jnp.float32)
    pl.semaphore_wait(barrier, len(peers))

    pair_copy = remote(both.at[core], both.at[core], pair_sem.at[0], pair_sem.at[1], sibling)
    pair_copy.start()
    mark_copy = remote(marks_ref, other_marks, mark_sem.at[0], mark_sem.at[1], across)
    mark_copy.start()
    pair_copy.wait()

    def columns(step):
        return pl.ds(pl.multiple_of((2 * step + core) * SLAB, SLAB), SLAB)

    def z_copy(step, d):
        block = rows.at[0, z, y, :, columns(step)]
        return remote(block, block, z_sem.at[0, d - 1, step], z_sem.at[1, d - 1, step], along(d))

    first = (
        (1 - core) * (1 - x) + core * x,
        z * 2 + (1 - core) * y + core * (1 - y),
        core,
    )
    second = (
        core * (1 - x) + (1 - core) * x,
        z * 2 + core * y + (1 - core) * (1 - y),
        core,
    )
    far_y = (1 - core) * y + core * (1 - y)

    def near_copy(step, kind):
        cols = columns(step)
        if kind == 0:
            src, dst, device = rows.at[0, :, y, :, cols], rows.at[1 - core, :, y, :, cols], first
        elif kind == 1:
            src, dst, device = rows.at[0, :, y, :, cols], rows.at[core, :, y, :, cols], second
        else:
            src = rows.at[1 - core, :, far_y, :, cols]
            dst, device = rows.at[1, :, far_y, :, cols], second
        return remote(src, dst, near_sem.at[0, kind, step], near_sem.at[1, kind, step], device)

    def sib_copy(step):
        block = rows.at[:, :, :, :, columns(step)]
        return remote(block, block, sib_sem.at[0, step], sib_sem.at[1, step], sibling)

    @pl.loop(0, pairs)
    def _(step):
        rows[0, z, y, :, columns(step)] = (
            both[:, :, columns(step)].reshape(16, SLAB).astype(jnp.bfloat16)
        )
        for d in (1, 2, 3):
            z_copy(step, d).start()

    @pl.loop(0, pairs + 3)
    def _(i):
        @pl.when(i < pairs)
        def _():
            for d in (1, 2, 3):
                z_copy(i, d).wait_recv()
            near_copy(i, 0).start()
            near_copy(i, 1).start()

        @pl.when((i >= 1) & (i < pairs + 1))
        def _():
            near_copy(i - 1, 0).wait_recv()
            near_copy(i - 1, 2).start()

        @pl.when((i >= 2) & (i < pairs + 2))
        def _():
            near_copy(i - 2, 1).wait_recv()
            near_copy(i - 2, 2).wait_recv()
            sib_copy(i - 2).start()

        @pl.when(i >= 3)
        def _():
            p = i - 3
            sib_copy(p).wait_recv()
            load(p).wait()
            slot = p % SLOTS
            right = rows[:, :, :, :, pl.ds(pl.multiple_of(p * PAIR, PAIR), PAIR)].reshape(-1, PAIR)

            def product(t):
                at = pl.ds(pl.multiple_of(t * TILE, TILE), TILE)
                return at, lax.dot_general(
                    ring[slot, at, :], right, (((1,), (1,)), ((), ())),
                    preferred_element_type=jnp.float32,
                )

            @pl.when(p == 0)
            def _():
                @pl.loop(0, tiles)
                def _(t):
                    at, term = product(t)
                    logits[at, :] = term

            @pl.when(p > 0)
            def _():
                @pl.loop(0, tiles)
                def _(t):
                    at, term = product(t)
                    logits[at, :] += term

            @pl.when(p + SLOTS < pairs)
            def _():
                load(p + SLOTS).start()

    rows_copy = pltpu.make_async_copy(
        rows.at[:, :, :, :, pl.ds(pl.multiple_of(x * half, 128), half)], rows_out, out_sem.at[0]
    )
    rows_copy.start()

    count = logits.shape[1]

    def top(t, best):
        at = pl.ds(pl.multiple_of(t * TILE, TILE), TILE)
        return jnp.maximum(best, jnp.max(logits[at, :].reshape(TILE // 8, 8, count), axis=0))

    best = lax.fori_loop(0, tiles, top, jnp.full((8, count), -jnp.inf, jnp.float32))
    peak = jnp.max(best, axis=0, keepdims=True)

    def accumulate(t, total):
        at = pl.ds(pl.multiple_of(t * TILE, TILE), TILE)
        e = jnp.exp(logits[at, :] - peak)
        logits[at, :] = e
        return total + jnp.sum(e.reshape(TILE // 8, 8, count), axis=0)

    part = lax.fori_loop(0, tiles, accumulate, jnp.zeros((8, count), jnp.float32))
    part = jnp.sum(part, axis=0, keepdims=True)

    def stat_copy(stage, slot, device):
        return remote(
            stat_out.at[stage], stat_in.at[slot], stat_sem.at[0, slot], stat_sem.at[1, slot], device
        )

    row_peak, row_sum = peak, part
    slot = 0
    stat_copies = []
    for stage, devices in enumerate(([sibling], [beside], [along(1), along(2), along(3)])):
        stat_out[stage, 0:8] = jnp.broadcast_to(row_peak, (8, count))
        stat_out[stage, 8:16] = jnp.broadcast_to(row_sum, (8, count))
        copies = [stat_copy(stage, slot + i, device) for i, device in enumerate(devices)]
        for copy in copies:
            copy.start()
        for i, copy in enumerate(copies):
            copy.wait_recv()
            got_peak, got_sum = stat_in[slot + i, 0:1], stat_in[slot + i, 8:9]
            new_peak = jnp.maximum(row_peak, got_peak)
            row_sum = row_sum * jnp.exp(row_peak - new_peak) + got_sum * jnp.exp(got_peak - new_peak)
            row_peak = new_peak
        slot += len(devices)
        stat_copies += copies
    factor = jnp.exp(peak - row_peak - jnp.log(row_sum))

    mark_copy.wait()
    label = jnp.concatenate([marks_ref[0:1], other_marks[0:1]], axis=1).astype(jnp.int32)
    weight = jnp.concatenate([marks_ref[1:2], other_marks[1:2]], axis=1)
    label = label - (dp * 2 + core) * vocab

    @pl.loop(0, tiles)
    def _(t):
        at = pl.ds(pl.multiple_of(t * TILE, TILE), TILE)
        entry = lax.broadcasted_iota(jnp.int32, (TILE, count), 0) + t * TILE
        hit = jnp.where(entry == label, 1.0, 0.0)
        g = weight * (logits[at, :] * factor - hit)
        grad_t[at, :] = g.astype(jnp.bfloat16)
        grad_o[:, at] = g[:, count // 2 :].T.astype(jnp.bfloat16)

    grad_copy = pltpu.make_async_copy(grad_t, grad_out, out_sem.at[1])
    grad_copy.start()

    def give(i):
        return remote(sent.at[i], got.at[i], back_sem.at[0, 0, i], back_sem.at[1, 0, i], sibling)

    def give_y(i):
        return remote(y_sent.at[i], y_got.at[i], back_sem.at[0, 1, i], back_sem.at[1, 1, i], beside)

    def give_z(i, d):
        return remote(
            z_sent.at[i, (z + d) % 4], z_got.at[i, d - 1],
            back_sem.at[0, 1 + d, i], back_sem.at[1, 1 + d, i], along(d),
        )

    @pl.loop(0, pairs + 3)
    def _(i):
        @pl.when(i < pairs)
        def _():
            p = pairs - 1 - i

            @pl.when(p < pairs - SLOTS)
            def _():
                load(p).wait()

            slot = p % SLOTS

            def dot(which):
                cols = pl.ds(pl.multiple_of(which * SLAB, SLAB), SLAB)
                return jnp.dot(grad_o[...], ring[slot, :, cols], preferred_element_type=jnp.float32)

            sent[i] = dot(1 - core).reshape(4, 2, 16, SLAB)
            give(i).start()
            mine[i] = dot(core).reshape(4, 2, 16, SLAB)

            @pl.when(p >= SLOTS)
            def _():
                load(p - SLOTS).start()

        @pl.when((i >= 1) & (i < pairs + 1))
        def _():
            j = i - 1
            give(j).wait_recv()
            y_sent[j] = (mine[j, :, 1 - y] + got[j, :, 1 - y]).astype(jnp.bfloat16)
            give_y(j).start()
            y_part[j] = mine[j, :, y] + got[j, :, y]

        @pl.when((i >= 2) & (i < pairs + 2))
        def _():
            j = i - 2
            give_y(j).wait_recv()
            total = y_part[j] + y_got[j].astype(jnp.float32)
            y_part[j] = total
            z_sent[j] = total.astype(jnp.bfloat16)
            for d in (1, 2, 3):
                give_z(j, d).start()

        @pl.when(i >= 3)
        def _():
            j = i - 3
            total = y_part[j, z]
            for d in (1, 2, 3):
                give_z(j, d).wait_recv()
                total = total + z_got[j, d - 1].astype(jnp.float32)
            final[0, pairs - 1 - j] = total[0:8]
            final[1, pairs - 1 - j] = total[8:16]

    last = remote(final.at[1 - core], cross, last_sem.at[0], last_sem.at[1], sibling)
    last.start()
    last.wait()
    sum_out[core] = final[core]
    sum_out[1 - core] = cross[...]

    for copy in stat_copies:
        copy.wait_send()

    @pl.loop(0, pairs)
    def _(i):
        for d in (1, 2, 3):
            z_copy(i, d).wait_send()
            give_z(i, d).wait_send()
        for kind in (0, 1, 2):
            near_copy(i, kind).wait_send()
        sib_copy(i).wait_send()
        give(i).wait_send()
        give_y(i).wait_send()

    rows_copy.wait()
    grad_copy.wait()


def fused_plan(hidden, gain, table, labels, token_weight):
    section = lax.axis_index("section")
    tokens = labels.shape[1]
    vocab, width = table.shape
    half, pairs = width // 2, width // PAIR
    own = hidden.shape[1]
    other_rows = lax.ppermute(hidden[0], "section", [(0, 1), (1, 0)])
    marks = jnp.concatenate(
        [labels.astype(jnp.float32), token_weight, jnp.zeros((6, tokens), jnp.float32)], axis=0
    )
    f32, b16, sem = jnp.float32, jnp.bfloat16, pltpu.SemaphoreType.DMA
    vmem, anywhere = pl.BlockSpec(memory_space=pltpu.VMEM), pl.BlockSpec(memory_space=pl.ANY)
    grad_t, rows, sums = pl.pallas_call(
        fused_kernel,
        out_shape=(
            jax.ShapeDtypeStruct((vocab, 2 * tokens), b16),
            jax.ShapeDtypeStruct((2, 4, 2, 16, half), b16),
            jax.ShapeDtypeStruct((2, pairs, own, SLAB), f32),
        ),
        in_specs=[vmem, vmem, anywhere, vmem],
        out_specs=(anywhere, anywhere, vmem),
        scratch_shapes=[
            pltpu.VMEM((2, 4, 2, 16, width), b16),
            pltpu.VMEM((2, own, width), f32),
            pltpu.VMEM((8, tokens), f32),
            pltpu.VMEM((SLOTS, vocab, PAIR), b16),
            pltpu.VMEM((vocab, 2 * tokens), f32),
            pltpu.VMEM((vocab, 2 * tokens), b16),
            pltpu.VMEM((tokens, vocab), b16),
            pltpu.VMEM((3, 16, 2 * tokens), f32),
            pltpu.VMEM((5, 16, 2 * tokens), f32),
            pltpu.VMEM((pairs, 4, 2, 16, SLAB), f32),
            pltpu.VMEM((pairs, 4, 2, 16, SLAB), f32),
            pltpu.VMEM((pairs, 4, 2, 16, SLAB), f32),
            pltpu.VMEM((pairs, 4, 16, SLAB), f32),
            pltpu.VMEM((pairs, 4, 16, SLAB), b16),
            pltpu.VMEM((pairs, 4, 16, SLAB), b16),
            pltpu.VMEM((pairs, 4, 16, SLAB), b16),
            pltpu.VMEM((pairs, 3, 16, SLAB), b16),
            pltpu.VMEM((2, pairs, own, SLAB), f32),
            pltpu.VMEM((pairs, own, SLAB), f32),
            sem((SLOTS,)),
            sem((2,)),
            sem((2,)),
            sem((2,)),
            sem((2, 3, pairs)),
            sem((2, 3, pairs)),
            sem((2, pairs)),
            sem((2, 5)),
            sem((2, 5, pairs)),
            sem((2,)),
        ],
        compiler_params=pltpu.CompilerParams(
            collective_id=0, has_side_effects=True, vmem_limit_bytes=60 * 2**20
        ),
        cost_estimate=pl.CostEstimate(
            flops=6 * tokens * vocab * width, bytes_accessed=3 * vocab * width, transcendentals=0
        ),
    )(hidden[0], gain[None], table, marks)
    table_grad = jnp.einsum(
        "vt,td->vd", grad_t, rows.reshape(2 * tokens, half), preferred_element_type=f32
    ).astype(b16)
    normed_grad = jnp.transpose(sums, (2, 1, 0, 3)).reshape(own, width)
    inverse, unit, _ = normalize(other_rows, gain)
    scaled = normed_grad * gain
    section_grad = (
        inverse * (scaled - unit * jnp.mean(scaled * unit, axis=1, keepdims=True))
    ).astype(b16)
    return (section_grad[None], table_grad)


def plain_plan(hidden, gain, table, labels, token_weight):
    section = lax.axis_index("section")
    tokens = labels.shape[1]
    vocab_rows, width = table.shape
    half = width // 2
    normed_own = normalize(hidden[0], gain)[2]
    normed = lax.all_gather(normed_own, ("section", "dp", "tensor"), axis=0, tiled=True)
    other_rows = lax.ppermute(hidden[0], "section", [(0, 1), (1, 0)])
    labels_all = lax.all_gather(labels[0], "section", axis=0, tiled=True)
    weight_all = lax.all_gather(token_weight[0], "section", axis=0, tiled=True)
    logits = jnp.einsum("td,vd->tv", normed, table, preferred_element_type=jnp.float32)
    peak = jnp.max(logits, axis=1)
    part = jnp.sum(jnp.exp(logits - peak[:, None]), axis=1)
    stats = lax.all_gather(jnp.stack([peak, part]), ("dp", "tensor"), axis=0)
    row_peak = jnp.max(stats[:, 0], axis=0)
    row_sum = jnp.sum(stats[:, 1] * jnp.exp(stats[:, 0] - row_peak[None]), axis=0)
    log_total = row_peak + jnp.log(row_sum)
    first_entry = lax.axis_index(("dp", "tensor")) * vocab_rows
    entries = first_entry + jnp.arange(vocab_rows, dtype=jnp.int32)
    is_label = (entries[None, :] == labels_all[:, None]).astype(jnp.float32)
    logit_grad = (
        weight_all[:, None] * (jnp.exp(logits - log_total[:, None]) - is_label)
    ).astype(jnp.bfloat16)
    other_grad = lax.dynamic_slice_in_dim(logit_grad, (1 - section) * tokens, tokens, axis=0)
    normed_grad = lax.psum_scatter(
        jnp.dot(other_grad, table, preferred_element_type=jnp.float32),
        ("dp", "tensor"),
        scatter_dimension=0,
        tiled=True,
    )
    own_columns = lax.dynamic_slice_in_dim(normed, section * half, half, axis=1)
    table_grad = jnp.einsum(
        "tv,td->vd", logit_grad, own_columns, preferred_element_type=jnp.float32
    ).astype(jnp.bfloat16)
    inverse, unit, _ = normalize(other_rows, gain)
    scaled = normed_grad * gain
    section_grad = (
        inverse * (scaled - unit * jnp.mean(scaled * unit, axis=1, keepdims=True))
    ).astype(jnp.bfloat16)
    return (section_grad[None], table_grad)


def solution(mesh):
    in_specs = (
        P("section", ("dp", "tensor"), None),
        P(),
        P(("dp", "tensor"), None),
        P("section", None),
        P("section", None),
    )
    out_specs = (P("section", ("dp", "tensor"), None), P(("dp", "tensor"), "section"))
    sizes = (mesh.shape["section"], mesh.shape["dp"], mesh.shape["tensor"])

    def on_device(hidden, gain, table, labels, token_weight):
        fits = (
            sizes == (2, 8, 2)
            and hidden.shape[1] == 8
            and table.shape[0] == 4096
            and table.shape[1] % (2 * PAIR) == PAIR
        )
        plan = fused_plan if fits else plain_plan
        return plan(hidden, gain, table, labels, token_weight)

    return jax.shard_map(
        on_device, mesh=mesh, in_specs=in_specs, out_specs=out_specs, check_vma=False
    )
```

```python
import jax
import jax.numpy as jnp
from jax import lax
from jax.experimental import pallas as pl
from jax.experimental.pallas import tpu as pltpu
from jax.sharding import PartitionSpec as P


def normalize(source_rows, gain):
    values = source_rows.astype(jnp.float32)
    inverse = lax.rsqrt(jnp.mean(values * values, axis=1, keepdims=True) + 1e-06)
    unit = values * inverse
    return (inverse, unit, (unit * gain).astype(jnp.bfloat16))


MESH = pl.DeviceIdType.MESH
PAIR = 1024
SLAB = 512
SLOTS = 4
TILE = 512
ROWS = 256


def fused_kernel(
    hidden_ref, gain_ref, table_ref, marks_ref,
    grad_out, rows_out, sum_out,
    rows, both, other_marks, ring, logits, grad_t, grad_o, stat_out, stat_in,
    mine, sent, got, y_part, y_sent, y_got, z_sent, z_got, final, cross,
    ring_sem, out_sem, pair_sem, mark_sem, z_sem, near_sem, sib_sem, stat_sem,
    back_sem, last_sem,
):
    x = lax.axis_index("section")
    dp = lax.axis_index("dp")
    core = lax.axis_index("tensor")
    z, y = dp // 2, dp % 2
    pairs = table_ref.shape[1] // PAIR
    vocab = table_ref.shape[0]
    half = rows_out.shape[4]
    tiles = vocab // TILE

    sibling = {"tensor": 1 - core}
    across = {"section": 1 - x}
    beside = {"dp": z * 2 + (1 - y)}

    def along(step):
        return {"dp": ((z + step) % 4) * 2 + y}

    def load(pair):
        return pltpu.make_async_copy(
            table_ref.at[:, pl.ds(pl.multiple_of(pair * PAIR, PAIR), PAIR)],
            ring.at[pair % SLOTS],
            ring_sem.at[pair % SLOTS],
        )

    for pair in range(SLOTS):
        load(pair).start()

    def remote(src, dst, send, recv, device):
        return pltpu.make_async_remote_copy(
            src_ref=src, dst_ref=dst, send_sem=send, recv_sem=recv,
            device_id=device, device_id_type=MESH,
        )

    barrier = pltpu.get_barrier_semaphore()
    peers = [sibling, across, beside, along(1), along(2), along(3)]
    for peer in peers:
        pl.semaphore_signal(barrier, inc=1, device_id=peer, device_id_type=MESH)

    values = hidden_ref[...].astype(jnp.float32)
    inverse = lax.rsqrt(jnp.mean(values * values, axis=1, keepdims=True) + 1e-06)
    normed = (values * inverse * gain_ref[...]).astype(jnp.bfloat16)
    both[core] = normed.astype(jnp.float32)
    pl.semaphore_wait(barrier, len(peers))

    pair_copy = remote(both.at[core], both.at[core], pair_sem.at[0], pair_sem.at[1], sibling)
    pair_copy.start()
    mark_copy = remote(marks_ref, other_marks, mark_sem.at[0], mark_sem.at[1], across)
    mark_copy.start()
    pair_copy.wait()

    def columns(step):
        return pl.ds(pl.multiple_of((2 * step + core) * SLAB, SLAB), SLAB)

    def z_copy(step, d):
        block = rows.at[0, z, y, :, columns(step)]
        return remote(block, block, z_sem.at[0, d - 1, step], z_sem.at[1, d - 1, step], along(d))

    first = (
        (1 - core) * (1 - x) + core * x,
        z * 2 + (1 - core) * y + core * (1 - y),
        core,
    )
    second = (
        core * (1 - x) + (1 - core) * x,
        z * 2 + core * y + (1 - core) * (1 - y),
        core,
    )
    far_y = (1 - core) * y + core * (1 - y)

    def near_copy(step, kind):
        cols = columns(step)
        if kind == 0:
            src, dst, device = rows.at[0, :, y, :, cols], rows.at[1 - core, :, y, :, cols], first
        elif kind == 1:
            src, dst, device = rows.at[0, :, y, :, cols], rows.at[core, :, y, :, cols], second
        else:
            src = rows.at[1 - core, :, far_y, :, cols]
            dst, device = rows.at[1, :, far_y, :, cols], second
        return remote(src, dst, near_sem.at[0, kind, step], near_sem.at[1, kind, step], device)

    def sib_copy(step):
        block = rows.at[:, :, :, :, columns(step)]
        return remote(block, block, sib_sem.at[0, step], sib_sem.at[1, step], sibling)

    @pl.loop(0, pairs)
    def _(step):
        rows[0, z, y, :, columns(step)] = (
            both[:, :, columns(step)].reshape(16, SLAB).astype(jnp.bfloat16)
        )
        for d in (1, 2, 3):
            z_copy(step, d).start()

    @pl.loop(0, pairs + 3)
    def _(i):
        @pl.when(i < pairs)
        def _():
            for d in (1, 2, 3):
                z_copy(i, d).wait_recv()
            near_copy(i, 0).start()
            near_copy(i, 1).start()

        @pl.when((i >= 1) & (i < pairs + 1))
        def _():
            near_copy(i - 1, 0).wait_recv()
            near_copy(i - 1, 2).start()

        @pl.when((i >= 2) & (i < pairs + 2))
        def _():
            near_copy(i - 2, 1).wait_recv()
            near_copy(i - 2, 2).wait_recv()
            sib_copy(i - 2).start()

        @pl.when(i >= 3)
        def _():
            p = i - 3
            sib_copy(p).wait_recv()
            load(p).wait()
            slot = p % SLOTS
            right = rows[:, :, :, :, pl.ds(pl.multiple_of(p * PAIR, PAIR), PAIR)].reshape(-1, PAIR)

            def product(t):
                at = pl.ds(pl.multiple_of(t * TILE, TILE), TILE)
                return at, lax.dot_general(
                    ring[slot, at, :], right, (((1,), (1,)), ((), ())),
                    preferred_element_type=jnp.float32,
                )

            @pl.when(p == 0)
            def _():
                @pl.loop(0, tiles)
                def _(t):
                    at, term = product(t)
                    logits[at, :] = term

            @pl.when(p > 0)
            def _():
                @pl.loop(0, tiles)
                def _(t):
                    at, term = product(t)
                    logits[at, :] += term

            @pl.when(p + SLOTS < pairs)
            def _():
                load(p + SLOTS).start()

    rows_copy = pltpu.make_async_copy(
        rows.at[:, :, :, :, pl.ds(pl.multiple_of(x * half, 128), half)], rows_out, out_sem.at[0]
    )
    rows_copy.start()

    count = logits.shape[1]

    def top(t, best):
        at = pl.ds(pl.multiple_of(t * TILE, TILE), TILE)
        return jnp.maximum(best, jnp.max(logits[at, :].reshape(TILE // 8, 8, count), axis=0))

    best = lax.fori_loop(0, tiles, top, jnp.full((8, count), -jnp.inf, jnp.float32))
    peak = jnp.max(best, axis=0, keepdims=True)

    def accumulate(t, total):
        at = pl.ds(pl.multiple_of(t * TILE, TILE), TILE)
        e = jnp.exp(logits[at, :] - peak)
        logits[at, :] = e
        return total + jnp.sum(e.reshape(TILE // 8, 8, count), axis=0)

    part = lax.fori_loop(0, tiles, accumulate, jnp.zeros((8, count), jnp.float32))
    part = jnp.sum(part, axis=0, keepdims=True)

    def stat_copy(stage, slot, device):
        return remote(
            stat_out.at[stage], stat_in.at[slot], stat_sem.at[0, slot], stat_sem.at[1, slot], device
        )

    row_peak, row_sum = peak, part
    slot = 0
    stat_copies = []
    for stage, devices in enumerate(([sibling], [beside], [along(1), along(2), along(3)])):
        stat_out[stage, 0:8] = jnp.broadcast_to(row_peak, (8, count))
        stat_out[stage, 8:16] = jnp.broadcast_to(row_sum, (8, count))
        copies = [stat_copy(stage, slot + i, device) for i, device in enumerate(devices)]
        for copy in copies:
            copy.start()
        for i, copy in enumerate(copies):
            copy.wait_recv()
            got_peak, got_sum = stat_in[slot + i, 0:1], stat_in[slot + i, 8:9]
            new_peak = jnp.maximum(row_peak, got_peak)
            row_sum = row_sum * jnp.exp(row_peak - new_peak) + got_sum * jnp.exp(got_peak - new_peak)
            row_peak = new_peak
        slot += len(devices)
        stat_copies += copies
    factor = jnp.exp(peak - row_peak - jnp.log(row_sum))

    mark_copy.wait()
    label = jnp.concatenate([marks_ref[0:1], other_marks[0:1]], axis=1).astype(jnp.int32)
    weight = jnp.concatenate([marks_ref[1:2], other_marks[1:2]], axis=1)
    label = label - (dp * 2 + core) * vocab

    @pl.loop(0, tiles)
    def _(t):
        at = pl.ds(pl.multiple_of(t * TILE, TILE), TILE)
        entry = lax.broadcasted_iota(jnp.int32, (TILE, count), 0) + t * TILE
        hit = jnp.where(entry == label, 1.0, 0.0)
        g = weight * (logits[at, :] * factor - hit)
        grad_t[at, :] = g.astype(jnp.bfloat16)
        grad_o[:, at] = g[:, count // 2 :].T.astype(jnp.bfloat16)

    grad_copy = pltpu.make_async_copy(grad_t, grad_out, out_sem.at[1])
    grad_copy.start()

    def give(i):
        return remote(sent.at[i], got.at[i], back_sem.at[0, 0, i], back_sem.at[1, 0, i], sibling)

    def give_y(i):
        return remote(y_sent.at[i], y_got.at[i], back_sem.at[0, 1, i], back_sem.at[1, 1, i], beside)

    def give_z(i, d):
        return remote(
            z_sent.at[i, (z + d) % 4], z_got.at[i, d - 1],
            back_sem.at[0, 1 + d, i], back_sem.at[1, 1 + d, i], along(d),
        )

    @pl.loop(0, pairs + 3)
    def _(i):
        @pl.when(i < pairs)
        def _():
            p = pairs - 1 - i

            @pl.when(p < pairs - SLOTS)
            def _():
                load(p).wait()

            slot = p % SLOTS

            def dot(which):
                cols = pl.ds(pl.multiple_of(which * SLAB, SLAB), SLAB)
                return jnp.dot(grad_o[...], ring[slot, :, cols], preferred_element_type=jnp.float32)

            sent[i] = dot(1 - core).reshape(4, 2, 16, SLAB)
            give(i).start()
            mine[i] = dot(core).reshape(4, 2, 16, SLAB)

            @pl.when(p >= SLOTS)
            def _():
                load(p - SLOTS).start()

        @pl.when((i >= 1) & (i < pairs + 1))
        def _():
            j = i - 1
            give(j).wait_recv()
            y_sent[j] = (mine[j, :, 1 - y] + got[j, :, 1 - y]).astype(jnp.bfloat16)
            give_y(j).start()
            y_part[j] = mine[j, :, y] + got[j, :, y]

        @pl.when((i >= 2) & (i < pairs + 2))
        def _():
            j = i - 2
            give_y(j).wait_recv()
            total = y_part[j] + y_got[j].astype(jnp.float32)
            y_part[j] = total
            z_sent[j] = total.astype(jnp.bfloat16)
            for d in (1, 2, 3):
                give_z(j, d).start()

        @pl.when(i >= 3)
        def _():
            j = i - 3
            total = y_part[j, z]
            for d in (1, 2, 3):
                give_z(j, d).wait_recv()
                total = total + z_got[j, d - 1].astype(jnp.float32)
            final[0, pairs - 1 - j] = total[0:8]
            final[1, pairs - 1 - j] = total[8:16]

    last = remote(final.at[1 - core], cross, last_sem.at[0], last_sem.at[1], sibling)
    last.start()
    last.wait()
    sum_out[core] = final[core]
    sum_out[1 - core] = cross[...]

    for copy in stat_copies:
        copy.wait_send()

    @pl.loop(0, pairs)
    def _(i):
        for d in (1, 2, 3):
            z_copy(i, d).wait_send()
            give_z(i, d).wait_send()
        for kind in (0, 1, 2):
            near_copy(i, kind).wait_send()
        sib_copy(i).wait_send()
        give(i).wait_send()
        give_y(i).wait_send()

    rows_copy.wait()
    grad_copy.wait()


def weight_kernel(grad_ref, rows_ref, out_ref):
    out_ref[...] = jnp.dot(
        grad_ref[...], rows_ref[...], preferred_element_type=jnp.float32
    ).astype(out_ref.dtype)


def fused_plan(hidden, gain, table, labels, token_weight):
    section = lax.axis_index("section")
    tokens = labels.shape[1]
    vocab, width = table.shape
    half, pairs = width // 2, width // PAIR
    own = hidden.shape[1]
    other_rows = lax.ppermute(hidden[0], "section", [(0, 1), (1, 0)])
    marks = jnp.concatenate(
        [labels.astype(jnp.float32), token_weight, jnp.zeros((6, tokens), jnp.float32)], axis=0
    )
    f32, b16, sem = jnp.float32, jnp.bfloat16, pltpu.SemaphoreType.DMA
    vmem, anywhere = pl.BlockSpec(memory_space=pltpu.VMEM), pl.BlockSpec(memory_space=pl.ANY)
    grad_t, rows, sums = pl.pallas_call(
        fused_kernel,
        out_shape=(
            jax.ShapeDtypeStruct((vocab, 2 * tokens), b16),
            jax.ShapeDtypeStruct((2, 4, 2, 16, half), b16),
            jax.ShapeDtypeStruct((2, pairs, own, SLAB), f32),
        ),
        in_specs=[vmem, vmem, anywhere, vmem],
        out_specs=(anywhere, anywhere, vmem),
        scratch_shapes=[
            pltpu.VMEM((2, 4, 2, 16, width), b16),
            pltpu.VMEM((2, own, width), f32),
            pltpu.VMEM((8, tokens), f32),
            pltpu.VMEM((SLOTS, vocab, PAIR), b16),
            pltpu.VMEM((vocab, 2 * tokens), f32),
            pltpu.VMEM((vocab, 2 * tokens), b16),
            pltpu.VMEM((tokens, vocab), b16),
            pltpu.VMEM((3, 16, 2 * tokens), f32),
            pltpu.VMEM((5, 16, 2 * tokens), f32),
            pltpu.VMEM((pairs, 4, 2, 16, SLAB), f32),
            pltpu.VMEM((pairs, 4, 2, 16, SLAB), f32),
            pltpu.VMEM((pairs, 4, 2, 16, SLAB), f32),
            pltpu.VMEM((pairs, 4, 16, SLAB), f32),
            pltpu.VMEM((pairs, 4, 16, SLAB), b16),
            pltpu.VMEM((pairs, 4, 16, SLAB), b16),
            pltpu.VMEM((pairs, 4, 16, SLAB), b16),
            pltpu.VMEM((pairs, 3, 16, SLAB), b16),
            pltpu.VMEM((2, pairs, own, SLAB), f32),
            pltpu.VMEM((pairs, own, SLAB), f32),
            sem((SLOTS,)),
            sem((2,)),
            sem((2,)),
            sem((2,)),
            sem((2, 3, pairs)),
            sem((2, 3, pairs)),
            sem((2, pairs)),
            sem((2, 5)),
            sem((2, 5, pairs)),
            sem((2,)),
        ],
        compiler_params=pltpu.CompilerParams(
            collective_id=0, has_side_effects=True, vmem_limit_bytes=60 * 2**20
        ),
        cost_estimate=pl.CostEstimate(
            flops=6 * tokens * vocab * width, bytes_accessed=3 * vocab * width, transcendentals=0
        ),
    )(hidden[0], gain[None], table, marks)
    table_grad = pl.pallas_call(
        weight_kernel,
        grid=(vocab // ROWS,),
        out_shape=jax.ShapeDtypeStruct((vocab, half), b16),
        in_specs=[
            pl.BlockSpec((ROWS, 2 * tokens), lambda i: (i, 0)),
            pl.BlockSpec((2 * tokens, half), lambda i: (0, 0)),
        ],
        out_specs=pl.BlockSpec((ROWS, half), lambda i: (i, 0)),
        compiler_params=pltpu.CompilerParams(vmem_limit_bytes=48 * 2**20),
    )(grad_t, rows.reshape(2 * tokens, half))
    normed_grad = jnp.transpose(sums, (2, 1, 0, 3)).reshape(own, width)
    inverse, unit, _ = normalize(other_rows, gain)
    scaled = normed_grad * gain
    section_grad = (
        inverse * (scaled - unit * jnp.mean(scaled * unit, axis=1, keepdims=True))
    ).astype(b16)
    return (section_grad[None], table_grad)


def plain_plan(hidden, gain, table, labels, token_weight):
    section = lax.axis_index("section")
    tokens = labels.shape[1]
    vocab_rows, width = table.shape
    half = width // 2
    normed_own = normalize(hidden[0], gain)[2]
    normed = lax.all_gather(normed_own, ("section", "dp", "tensor"), axis=0, tiled=True)
    other_rows = lax.ppermute(hidden[0], "section", [(0, 1), (1, 0)])
    labels_all = lax.all_gather(labels[0], "section", axis=0, tiled=True)
    weight_all = lax.all_gather(token_weight[0], "section", axis=0, tiled=True)
    logits = jnp.einsum("td,vd->tv", normed, table, preferred_element_type=jnp.float32)
    peak = jnp.max(logits, axis=1)
    part = jnp.sum(jnp.exp(logits - peak[:, None]), axis=1)
    stats = lax.all_gather(jnp.stack([peak, part]), ("dp", "tensor"), axis=0)
    row_peak = jnp.max(stats[:, 0], axis=0)
    row_sum = jnp.sum(stats[:, 1] * jnp.exp(stats[:, 0] - row_peak[None]), axis=0)
    log_total = row_peak + jnp.log(row_sum)
    first_entry = lax.axis_index(("dp", "tensor")) * vocab_rows
    entries = first_entry + jnp.arange(vocab_rows, dtype=jnp.int32)
    is_label = (entries[None, :] == labels_all[:, None]).astype(jnp.float32)
    logit_grad = (
        weight_all[:, None] * (jnp.exp(logits - log_total[:, None]) - is_label)
    ).astype(jnp.bfloat16)
    other_grad = lax.dynamic_slice_in_dim(logit_grad, (1 - section) * tokens, tokens, axis=0)
    normed_grad = lax.psum_scatter(
        jnp.dot(other_grad, table, preferred_element_type=jnp.float32),
        ("dp", "tensor"),
        scatter_dimension=0,
        tiled=True,
    )
    own_columns = lax.dynamic_slice_in_dim(normed, section * half, half, axis=1)
    table_grad = jnp.einsum(
        "tv,td->vd", logit_grad, own_columns, preferred_element_type=jnp.float32
    ).astype(jnp.bfloat16)
    inverse, unit, _ = normalize(other_rows, gain)
    scaled = normed_grad * gain
    section_grad = (
        inverse * (scaled - unit * jnp.mean(scaled * unit, axis=1, keepdims=True))
    ).astype(jnp.bfloat16)
    return (section_grad[None], table_grad)


def solution(mesh):
    in_specs = (
        P("section", ("dp", "tensor"), None),
        P(),
        P(("dp", "tensor"), None),
        P("section", None),
        P("section", None),
    )
    out_specs = (P("section", ("dp", "tensor"), None), P(("dp", "tensor"), "section"))
    sizes = (mesh.shape["section"], mesh.shape["dp"], mesh.shape["tensor"])

    def on_device(hidden, gain, table, labels, token_weight):
        fits = (
            sizes == (2, 8, 2)
            and hidden.shape[1] == 8
            and table.shape[0] == 4096
            and table.shape[1] % (2 * PAIR) == PAIR
        )
        plan = fused_plan if fits else plain_plan
        return plan(hidden, gain, table, labels, token_weight)

    return jax.shard_map(
        on_device, mesh=mesh, in_specs=in_specs, out_specs=out_specs, check_vma=False
    )
```
